32 devices in a mesh: groups: 2 (over y), patch: 4 (over z), sub: 2 (over x), lane: 2 (over core).
Axes of the slice: x: 2, y: 2, z: 4, core: 2. Of those that a mesh axis runs over, the one named last changes fastest.
Arguments:
- node_latents: float32 [4096, 512], P(('groups', 'patch', 'sub')), parts along dimension 0, may hold values from -6 to 6
- edge_latents: bfloat16 [32768, 512], P(('groups', 'patch', 'sub', 'lane')), parts along dimension 0, may hold values from -6 to 6
- sender_slot: int32 [32768], P(('groups', 'patch', 'sub', 'lane')), parts along dimension 0, may hold values from 0 to 543, as said below
- receiver_slot: int32 [32768], P(('groups', 'patch', 'sub', 'lane')), parts along dimension 0, may hold values from 0 to 543
- near_send: int32 [32, 2, 128], P(('groups', 'patch', 'sub', 'lane')), parts along dimension 0, may hold values from 0 to 255, as said below
- far_send: int32 [32, 8, 4], P(('groups', 'patch', 'sub', 'lane')), parts along dimension 0, may hold values from 0 to 255, as said below
- w_edge_in: bfloat16 [1536, 512], replicated, may hold values from -0.15625 to 0.15625
- w_edge_out: bfloat16 [512, 512], replicated, may hold values from -0.25 to 0.25
- w_node_in: bfloat16 [1024, 512], replicated, may hold values from -0.1875 to 0.1875
- w_node_out: bfloat16 [512, 512], replicated, may hold values from -0.25 to 0.25
- edge_bias_in: float32 [512], replicated, may hold values from -3 to 3
- edge_bias_out: float32 [512], replicated, may hold values from -3 to 3
- edge_gain: float32 [512], replicated, may hold values from 0.5 to 1.5
- edge_shift: float32 [512], replicated, may hold values from -2 to 2
- node_bias_in: float32 [512], replicated, may hold values from -3 to 3
- node_bias_out: float32 [512], replicated, may hold values from -3 to 3
- node_gain: float32 [512], replicated, may hold values from 0.5 to 1.5
- node_shift: float32 [512], replicated, may hold values from -2 to 2
Outputs:
- node_new: float32 [4096, 512], P(('groups', 'patch', 'sub')), parts along dimension 0
- edge_new: bfloat16 [32768, 512], P(('groups', 'patch', 'sub', 'lane')), parts along dimension 0
The draws below stay inside these ranges and needn't reach their ends.
There are 2 independent parts, one for each index of `groups`. The reference program is written for one: setup_inputs(seed, part) draws one part's arguments, and reference() takes and returns one part's arrays. A program takes and returns all parts, laid end to end along the dimension named above; an argument that names none is the same for every part. Nothing has to cross between parts.
Inputs may be any that keep to these rules, and one draw needn't show every extreme that they name: On every device, each of its 544 slots is named by at least one sender_slot or receiver_slot entry of that device. `near_send`: the 128 entries of one list are distinct local rows. `far_send`: the 4 entries of one list are distinct local rows.
All inputs are finite; a program needn't handle non-finite values.
Results may differ from the reference program's by a relative error of at most 0.005.
Values may be sent and summed in bfloat16 or wider, within the bound.
A program may use at most 64 MiB of HBM per device.

```python
import jax
import jax.numpy as jnp
from jax import lax

D = 512
NODE_GRP = 256
EDGE_DEV = 1024
NEAR = 128
FAR = 4
PEERS = 8
DEVS = 16
GHOSTS = 544
NODES = 2048
EDGES = 16384
N_PATCH = 4
N_SUB = 2
N_LANE = 2


def endpoint_slots(key):

    def one_device(dev_key):
        cover_key, extra_key, order_key = jax.random.split(dev_key, 3)
        covering = jax.random.permutation(cover_key, GHOSTS).astype(jnp.int32)
        extra_slots = jax.random.randint(extra_key, (2 * EDGE_DEV - GHOSTS,), 0, GHOSTS, dtype=jnp.int32)
        endpoints = jnp.concatenate([covering, extra_slots])
        return jax.random.permutation(order_key, endpoints)
    dev_keys = jax.random.split(key, DEVS)
    return jax.vmap(one_device)(dev_keys)


def draw_sender_slot(key, part):
    table = endpoint_slots(jax.random.fold_in(key, 5))
    return table[:, :EDGE_DEV].reshape(-1).astype(jnp.int32)


def draw_receiver_slot(key, part):
    table = endpoint_slots(jax.random.fold_in(key, 5))
    return table[:, EDGE_DEV:].reshape(-1).astype(jnp.int32)


def draw_near_send(key, part):
    key = jax.random.fold_in(key, 11)
    list_keys = jax.random.split(key, DEVS * 2)
    picks = jax.vmap(lambda one_key: jax.random.permutation(one_key, NODE_GRP)[:NEAR])(list_keys)
    return picks.reshape(DEVS, 2, NEAR).astype(jnp.int32)


def draw_far_send(key, part):
    key = jax.random.fold_in(key, 13)
    list_keys = jax.random.split(key, DEVS * PEERS)
    picks = jax.vmap(lambda one_key: jax.random.permutation(one_key, NODE_GRP)[:FAR])(list_keys)
    return picks.reshape(DEVS, PEERS, FAR).astype(jnp.int32)


def block_scale(key, extent, pieces, least, high):
    def one(position, parts):
        steps = jax.random.uniform(jax.random.fold_in(jax.random.fold_in(key, 6), position), (parts,), jnp.float32, least / len(pieces), high / len(pieces))
        return jnp.repeat(jnp.exp(steps), extent[position] // parts).reshape((-1,) + (1,) * (len(extent) - position - 1))

    factor_of = one(*pieces[0])
    for cut in pieces[1:]:
        factor_of = factor_of * one(*cut)
    return factor_of


def gaussian(rng, shape, spread, limit, pieces=(), kind=jnp.bfloat16):
    drawn = jax.random.normal(rng, shape, jnp.float32) * spread
    if len(pieces) > 0:
        drawn = block_scale(rng, shape, pieces, -0.22, 0.18) * drawn
    return jnp.clip(drawn, min=-limit, max=limit).astype(kind)


def setup_inputs(seed: int = 0, part: int = 0) -> dict:
    streams_of = jax.random.split(jax.random.key(seed), 19)
    part_keys = jax.random.split(jax.random.fold_in(streams_of[18], part), 19)
    node_latents = gaussian(part_keys[0], (NODES, D), 1.0, 6.0, ((0, 8),), jnp.float32)
    edge_latents = gaussian(part_keys[1], (EDGES, D), 1.0, 6.0, ((0, 16),))
    sender_slot = draw_sender_slot(jax.random.fold_in(jax.random.fold_in(streams_of[18], part), 71), part)
    receiver_slot = draw_receiver_slot(jax.random.fold_in(jax.random.fold_in(streams_of[18], part), 71), part)
    near_send = draw_near_send(jax.random.fold_in(jax.random.fold_in(streams_of[18], part), 71), part)
    far_send = draw_far_send(jax.random.fold_in(jax.random.fold_in(streams_of[18], part), 71), part)
    w_edge_in = gaussian(streams_of[6], (3 * D, D), (3 * D) ** -0.5, 0.15625)
    w_edge_out = gaussian(streams_of[7], (D, D), D ** -0.5, 0.25)
    w_node_in = gaussian(streams_of[8], (2 * D, D), (2 * D) ** -0.5, 0.1875)
    w_node_out = gaussian(streams_of[9], (D, D), D ** -0.5, 0.25)
    edge_bias_in = gaussian(streams_of[10], (D,), 0.5, 3.0, (), jnp.float32)
    edge_bias_out = gaussian(streams_of[11], (D,), 0.5, 3.0, (), jnp.float32)
    edge_gain = jnp.clip(1.0 + 0.1 * jax.random.normal(streams_of[12], (D,), jnp.float32), 0.5, 1.5)
    edge_shift = gaussian(streams_of[13], (D,), 0.3, 2.0, (), jnp.float32)
    node_bias_in = gaussian(streams_of[14], (D,), 0.5, 3.0, (), jnp.float32)
    node_bias_out = gaussian(streams_of[15], (D,), 0.5, 3.0, (), jnp.float32)
    node_gain = jnp.clip(1.0 + 0.1 * jax.random.normal(streams_of[16], (D,), jnp.float32), 0.5, 1.5)
    node_shift = gaussian(streams_of[17], (D,), 0.3, 2.0, (), jnp.float32)
    return {"node_latents": node_latents, "edge_latents": edge_latents, "sender_slot": sender_slot, "receiver_slot": receiver_slot, "near_send": near_send, "far_send": far_send, "w_edge_in": w_edge_in, "w_edge_out": w_edge_out, "w_node_in": w_node_in, "w_node_out": w_node_out, "edge_bias_in": edge_bias_in, "edge_bias_out": edge_bias_out, "edge_gain": edge_gain, "edge_shift": edge_shift, "node_bias_in": node_bias_in, "node_bias_out": node_bias_out, "node_gain": node_gain, "node_shift": node_shift}


def norm_rows(values, gain_vec, shift_vec):
    average = lax.optimization_barrier(jnp.mean(values, axis=-1, keepdims=True))
    centred = values - average
    variance = lax.optimization_barrier(jnp.mean(centred * centred, axis=-1, keepdims=True))
    return centred * lax.rsqrt(variance + 1e-05) * gain_vec + shift_vec

def ghost_nodes(near_send, far_send):
    peer_count = N_PATCH * N_SUB
    device = jnp.arange(peer_count * N_LANE, dtype=jnp.int32)
    group = device // N_LANE
    lane_index = device % N_LANE
    patch_index = group // N_SUB
    sub_index = group % N_SUB
    local = jnp.arange(NODE_GRP, dtype=jnp.int32)
    own_ids = group[:, None] * NODE_GRP + local[None, :]
    prev_group = (patch_index + N_PATCH - 1) % N_PATCH * N_SUB + sub_index
    next_group = (patch_index + 1) % N_PATCH * N_SUB + sub_index
    from_prev = prev_group[:, None] * NODE_GRP + near_send[prev_group * N_LANE + lane_index, 0]
    from_next = next_group[:, None] * NODE_GRP + near_send[next_group * N_LANE + lane_index, 1]
    owners = jnp.arange(peer_count, dtype=jnp.int32)
    owner_dev = owners[None, :] * N_LANE + lane_index[:, None]
    far_ids = owners[None, :, None] * NODE_GRP + far_send[owner_dev, group[:, None], :]
    far_flat = far_ids.reshape(device.shape[0], peer_count * FAR)
    return jnp.concatenate([own_ids, from_prev, from_next, far_flat], axis=1).astype(jnp.int32)

def reference(node_latents, edge_latents, sender_slot, receiver_slot, near_send, far_send, w_edge_in, w_edge_out, w_node_in, w_node_out, edge_bias_in, edge_bias_out, edge_gain, edge_shift, node_bias_in, node_bias_out, node_gain, node_shift):
    feat_width = node_latents.shape[1]
    node_bf = node_latents.astype(jnp.bfloat16)
    proj_send = jnp.dot(node_bf, w_edge_in[feat_width:2 * feat_width], preferred_element_type=jnp.float32).astype(jnp.bfloat16)
    proj_recv = jnp.dot(node_bf, w_edge_in[2 * feat_width:], preferred_element_type=jnp.float32).astype(jnp.bfloat16)
    ghost_ids = ghost_nodes(near_send, far_send)
    device_count = ghost_ids.shape[0]
    edge_blocks = edge_latents.reshape(device_count, -1, feat_width)
    send_blocks = sender_slot.reshape(device_count, -1)
    recv_blocks = receiver_slot.reshape(device_count, -1)

    def step(summed, items):
        edge_block, send_ids, recv_ids, ghost_row = items
        senders = ghost_row[send_ids]
        receivers = ghost_row[recv_ids]
        preact = jnp.dot(edge_block, w_edge_in[:feat_width], preferred_element_type=jnp.float32)
        preact = preact + proj_send[senders].astype(jnp.float32) + proj_recv[receivers].astype(jnp.float32) + edge_bias_in
        hidden = jax.nn.silu(preact).astype(jnp.bfloat16)
        message = norm_rows(jnp.dot(hidden, w_edge_out, preferred_element_type=jnp.float32) + edge_bias_out, edge_gain, edge_shift)
        updated = (edge_block.astype(jnp.float32) + message).astype(jnp.bfloat16)
        return (summed.at[receivers].add(message), updated)
    start = jnp.zeros((node_latents.shape[0], feat_width), jnp.float32)
    summed, updated = lax.scan(step, start, (edge_blocks, send_blocks, recv_blocks, ghost_ids))
    summed_bf = summed.astype(jnp.bfloat16)
    node_pre = jnp.dot(node_bf, w_node_in[:feat_width], preferred_element_type=jnp.float32)
    node_pre = node_pre + jnp.dot(summed_bf, w_node_in[feat_width:], preferred_element_type=jnp.float32) + node_bias_in
    node_hidden = jax.nn.silu(node_pre).astype(jnp.bfloat16)
    node_out = jnp.dot(node_hidden, w_node_out, preferred_element_type=jnp.float32) + node_bias_out
    node_new = node_latents + norm_rows(node_out, node_gain, node_shift)
    return (node_new, updated.reshape(-1, feat_width))
```

```python
import functools

import jax
import jax.numpy as jnp
from jax import lax
from jax.experimental import pallas as pl
from jax.experimental.pallas import tpu as pltpu
from jax.sharding import PartitionSpec as P

MESH = pl.DeviceIdType.MESH
F32 = jnp.float32
BF16 = jnp.bfloat16
LANES = 128
ROW_BLOCK = 256


def mm(a, b):
    return jnp.dot(a, b, preferred_element_type=F32)


def silu(v):
    half = 0.5 * v
    return half + half * jnp.tanh(half)


def norm_rows(values, gain_vec, shift_vec):
    average = jnp.mean(values, axis=-1, keepdims=True)
    centred = values - average
    variance = jnp.mean(centred * centred, axis=-1, keepdims=True)
    return centred * lax.rsqrt(variance + 1e-05) * gain_vec + shift_vec


def ones_where(mask):
    return jnp.where(mask, 1.0, 0.0).astype(BF16)


def iota(shape, dim):
    return lax.broadcasted_iota(jnp.int32, shape, dim)


def layer_kernel(
    dims,
    node_hbm, edge_hbm, wei_hbm, weo_hbm, wni_hbm, wno_hbm,
    snd_ref, rcv_ref, lend_ref,
    ebi, ebo, egain, eshift, nbi, nbo, ngain, nshift,
    node_out, edge_out,
    node_v, edge_v, wei, weo, wni, wno, node_bf,
    lend_sel, near_src, far_src, near_in, far_in,
    pick_own, pick_ghost, proj_own, proj_ghost, drop, pre, msg,
    near_bsrc, far_bsrc, near_back, far_back, lane_src, lane_in, own_sum,
    load_sem, store_sem, near_ssem, near_rsem, far_ssem, far_rsem,
    nback_ssem, nback_rsem, fback_ssem, fback_rsem, lane_ssem, lane_rsem,
):
    n_patch, n_sub, n_lane, near, far = dims
    peers = n_patch * n_sub
    far_rows = peers * far
    pack = far * (node_v.shape[1] // LANES)
    n_node, d = node_v.shape
    n_edge = edge_v.shape[0]
    col_parts = d // LANES

    loads = [
        pltpu.make_async_copy(src, dst, load_sem.at[i])
        for i, (src, dst) in enumerate(
            [(node_hbm, node_v), (wei_hbm, wei), (edge_hbm, edge_v),
             (weo_hbm, weo), (wni_hbm, wni), (wno_hbm, wno)]
        )
    ]
    for load in loads:
        load.start()

    p = lax.axis_index("patch")
    s = lax.axis_index("sub")
    ln = lax.axis_index("lane")
    g = p * n_sub + s
    nxt = lax.rem(p + 1, n_patch)
    prv = lax.rem(p + n_patch - 1, n_patch)
    other = n_lane - 1 - ln

    def each_peer(fn):
        if peers <= 16:
            for o in range(1, peers):
                fn(o)
        else:
            def body(o, c):
                fn(o)
                return c
            lax.fori_loop(1, peers, body, 0)

    def peer_id(q):
        return {"patch": lax.div(q, n_sub), "sub": lax.rem(q, n_sub)}

    barrier = pltpu.get_barrier_semaphore()

    def greet(o):
        pl.semaphore_signal(
            barrier, inc=1, device_id=peer_id(lax.rem(g + o, peers)), device_id_type=MESH
        )

    each_peer(greet)
    pl.semaphore_signal(barrier, inc=1, device_id={"lane": other}, device_id_type=MESH)

    def column_of(ref, start, width):
        row = ref[:, start:start + width]
        return jnp.transpose(jnp.broadcast_to(row, (LANES, width)))

    lent = 2 * near + far_rows
    for r0 in range(0, lent, LANES):
        col = column_of(lend_ref, r0, LANES)
        for c0 in range(0, n_node, LANES):
            lend_sel[r0:r0 + LANES, c0:c0 + LANES] = ones_where(
                col == iota((LANES, LANES), 1) + c0
            )

    def packer(j):
        r = iota((peers * pack, far_rows), 0)
        c = iota((peers * pack, far_rows), 1)
        return ones_where(r == c // far * pack + j * far + c % far)

    def unpacker(j):
        r = iota((far_rows, peers * pack), 0)
        c = iota((far_rows, peers * pack), 1)
        return ones_where(c == r // far * pack + j * far + r % far)

    def packed(rows):
        total = mm(packer(0), rows[:, :LANES])
        for j in range(1, col_parts):
            total = total + mm(packer(j), rows[:, j * LANES:(j + 1) * LANES])
        return total.astype(BF16)

    def unpacked(block):
        return jnp.concatenate(
            [mm(unpacker(j), block).astype(BF16) for j in range(col_parts)], axis=1
        )

    loads[0].wait()
    node_bf[...] = node_v[...].astype(BF16)
    near_src[...] = mm(lend_sel[:2 * near, :], node_bf[...]).astype(BF16)
    far_src[...] = packed(
        mm(lend_sel[2 * near:lent, :], node_bf[...]).astype(BF16)
    )

    pl.semaphore_wait(barrier, peers)

    def near_copy(i, src, dst, ssem, rsem, patch):
        return pltpu.make_async_remote_copy(
            src_ref=src.at[pl.ds(i * near, near)],
            dst_ref=dst.at[pl.ds(i * near, near)],
            send_sem=ssem.at[i],
            recv_sem=rsem.at[i],
            device_id={"patch": patch},
            device_id_type=MESH,
        )

    def far_copy(o, src, dst, ssem, rsem):
        q = lax.rem(g + o, peers)
        return pltpu.make_async_remote_copy(
            src_ref=src.at[pl.ds(pl.multiple_of(q * pack, pack), pack)],
            dst_ref=dst.at[pl.ds(pl.multiple_of(g * pack, pack), pack)],
            send_sem=ssem.at[o],
            recv_sem=rsem.at[o],
            device_id=peer_id(q),
            device_id_type=MESH,
        )

    def far_arrival(o, src, dst, ssem, rsem):
        q = lax.rem(g + peers - o, peers)
        return pltpu.make_async_remote_copy(
            src_ref=src.at[pl.ds(pl.multiple_of(q * pack, pack), pack)],
            dst_ref=dst.at[pl.ds(pl.multiple_of(q * pack, pack), pack)],
            send_sem=ssem.at[o],
            recv_sem=rsem.at[o],
            device_id=peer_id(q),
            device_id_type=MESH,
        )

    def keep_own(src, dst):
        at = pl.ds(pl.multiple_of(g * pack, pack), pack)
        dst[at, :] = src[at, :]

    ahead = near_copy(0, near_src, near_in, near_ssem, near_rsem, nxt)
    behind = near_copy(1, near_src, near_in, near_ssem, near_rsem, prv)
    each_peer(lambda o: far_copy(o, far_src, far_in, far_ssem, far_rsem).start())
    ahead.start()
    behind.start()
    keep_own(far_src, far_in)

    loads[1].wait()
    proj_own[:n_node, :] = mm(node_bf[...], wei[d:2 * d, :]).astype(BF16)
    proj_own[n_node:, :] = mm(node_bf[...], wei[2 * d:, :]).astype(BF16)
    first_near = n_node
    first_far = n_node + 2 * near
    far_cols = proj_ghost.shape[0] - 4 * near
    for e0 in range(0, n_edge, LANES):
        scol = column_of(snd_ref, e0, LANES)
        rcol = column_of(rcv_ref, e0, LANES)
        rows = slice(e0, e0 + LANES)
        lane_ids = iota((LANES, LANES), 1)
        for c0 in range(0, n_node, LANES):
            pick_own[rows, c0:c0 + LANES] = ones_where(scol == lane_ids + c0)
            pick_own[rows, n_node + c0:n_node + c0 + LANES] = ones_where(rcol == lane_ids + c0)
        for c0 in range(0, 2 * near, LANES):
            at = first_near + c0
            pick_ghost[rows, c0:c0 + LANES] = ones_where(scol == lane_ids + at)
            pick_ghost[rows, 2 * near + c0:2 * near + c0 + LANES] = ones_where(rcol == lane_ids + at)
        for c0 in range(0, far_cols, LANES):
            c = lane_ids + c0
            is_s = c < far_rows
            slot = jnp.where(is_s, scol, rcol)
            name = jnp.where(is_s, c, c - far_rows) + first_far
            pick_ghost[rows, 4 * near + c0:4 * near + c0 + LANES] = ones_where(slot == name)

    loads[2].wait()
    for e0 in range(0, n_edge, ROW_BLOCK):
        rows = slice(e0, e0 + ROW_BLOCK)
        pre[rows, :] = mm(edge_v[rows, :], wei[:d, :]) + mm(pick_own[rows, :], proj_own[...]) + ebi[...]

    rcv_row = rcv_ref[...]
    for r0, base, count in (
        (0, first_near, 2 * near), (2 * near, first_far, far_rows), (lent, 0, n_node)
    ):
        drop[r0:r0 + count, :] = ones_where(iota((count, n_edge), 0) + base == rcv_row)
    if far_cols > 2 * far_rows:
        proj_ghost[4 * near + 2 * far_rows:, :] = jnp.zeros((far_cols - 2 * far_rows, d), BF16)

    each_peer(lambda o: far_arrival(o, far_src, far_in, far_ssem, far_rsem).wait_recv())
    far_nodes = unpacked(far_in[...])
    proj_ghost[4 * near:4 * near + far_rows, :] = mm(far_nodes, wei[d:2 * d, :]).astype(BF16)
    proj_ghost[4 * near + far_rows:4 * near + 2 * far_rows, :] = mm(
        far_nodes, wei[2 * d:, :]
    ).astype(BF16)
    ahead.wait_recv()
    behind.wait_recv()
    proj_ghost[:2 * near, :] = mm(near_in[...], wei[d:2 * d, :]).astype(BF16)
    proj_ghost[2 * near:4 * near, :] = mm(near_in[...], wei[2 * d:, :]).astype(BF16)

    loads[3].wait()
    stores = []
    for i, e0 in enumerate(range(0, n_edge, ROW_BLOCK)):
        rows = slice(e0, e0 + ROW_BLOCK)
        hidden = silu(pre[rows, :] + mm(pick_ghost[rows, :], proj_ghost[...])).astype(BF16)
        message = norm_rows(mm(hidden, weo[...]) + ebo[...], egain[...], eshift[...])
        msg[rows, :] = message.astype(BF16)
        edge_v[rows, :] = (edge_v[rows, :].astype(F32) + message).astype(BF16)
        store = pltpu.make_async_copy(edge_v.at[rows], edge_out.at[rows], store_sem.at[i])
        store.start()
        stores.append(store)

    near_bsrc[...] = mm(drop[:2 * near, :], msg[...]).astype(BF16)
    back_prev = near_copy(0, near_bsrc, near_back, nback_ssem, nback_rsem, prv)
    back_next = near_copy(1, near_bsrc, near_back, nback_ssem, nback_rsem, nxt)
    back_prev.start()
    back_next.start()
    far_bsrc[...] = packed(mm(drop[2 * near:lent, :], msg[...]).astype(BF16))
    each_peer(lambda o: far_copy(o, far_bsrc, far_back, fback_ssem, fback_rsem).start())
    keep_own(far_bsrc, far_back)
    own_sum[...] = mm(drop[lent:, :], msg[...])

    loads[4].wait()
    loads[5].wait()
    node_pre = mm(node_bf[...], wni[:d, :]) + nbi[...]
    give = ones_where(iota((n_node, lent), 0) == lend_ref[:, :lent])

    each_peer(lambda o: far_arrival(o, far_bsrc, far_back, fback_ssem, fback_rsem).wait_recv())
    own_sum[...] += mm(give[:, 2 * near:], unpacked(far_back[...]))
    back_prev.wait_recv()
    back_next.wait_recv()
    lane_src[...] = (own_sum[...] + mm(give[:, :2 * near], near_back[...])).astype(BF16)
    swap = pltpu.make_async_remote_copy(
        src_ref=lane_src, dst_ref=lane_in, send_sem=lane_ssem, recv_sem=lane_rsem,
        device_id={"lane": other}, device_id_type=MESH,
    )
    swap.start()
    swap.wait_recv()
    summed = (lane_src[...].astype(F32) + lane_in[...].astype(F32)).astype(BF16)
    node_hidden = silu(node_pre + mm(summed, wni[d:, :])).astype(BF16)
    node_out[...] = node_v[...] + norm_rows(
        mm(node_hidden, wno[...]) + nbo[...], ngain[...], nshift[...]
    )

    ahead.wait_send()
    behind.wait_send()
    back_prev.wait_send()
    back_next.wait_send()
    swap.wait_send()
    each_peer(lambda o: far_copy(o, far_src, far_in, far_ssem, far_rsem).wait_send())
    each_peer(lambda o: far_copy(o, far_bsrc, far_back, fback_ssem, fback_rsem).wait_send())
    for store in stores:
        store.wait()


def per_device(
    node_latents, edge_latents, sender_slot, receiver_slot, near_send, far_send,
    w_edge_in, w_edge_out, w_node_in, w_node_out,
    edge_bias_in, edge_bias_out, edge_gain, edge_shift,
    node_bias_in, node_bias_out, node_gain, node_shift,
):
    n_node, d = node_latents.shape
    n_edge = edge_latents.shape[0]
    near = near_send.shape[2]
    peers, far = far_send.shape[1:]
    n_patch, n_sub, n_lane = (lax.axis_size(a) for a in ("patch", "sub", "lane"))
    far_rows = peers * far
    lent = 2 * near + far_rows
    lent_pad = -(-lent // LANES) * LANES
    ghost_k = 4 * near + -(-2 * far_rows // LANES) * LANES
    pack = far * (d // LANES)
    blocks = n_edge // ROW_BLOCK
    lend = jnp.concatenate(
        [near_send.reshape(1, -1), far_send.reshape(1, -1),
         jnp.zeros((1, lent_pad - lent), jnp.int32)], axis=1
    )
    vectors = [v.reshape(1, d) for v in (
        edge_bias_in, edge_bias_out, edge_gain, edge_shift,
        node_bias_in, node_bias_out, node_gain, node_shift)]
    hbm = pl.BlockSpec(memory_space=pl.ANY)
    vmem = pl.BlockSpec(memory_space=pltpu.VMEM)
    dma = pltpu.SemaphoreType.DMA
    far_shape = (peers * pack, LANES)
    macs = n_edge * d * (3 * d + ghost_k + lent + n_node) + n_node * d * 6 * d
    return tuple(pl.pallas_call(
        functools.partial(layer_kernel, (n_patch, n_sub, n_lane, near, far)),
        out_shape=(
            jax.ShapeDtypeStruct((n_node, d), F32),
            jax.ShapeDtypeStruct((n_edge, d), BF16),
        ),
        in_specs=[hbm] * 6 + [vmem] * (3 + len(vectors)),
        out_specs=(vmem, hbm),
        scratch_shapes=[
            pltpu.VMEM((n_node, d), F32),
            pltpu.VMEM((n_edge, d), BF16),
            pltpu.VMEM(w_edge_in.shape, BF16),
            pltpu.VMEM(w_edge_out.shape, BF16),
            pltpu.VMEM(w_node_in.shape, BF16),
            pltpu.VMEM(w_node_out.shape, BF16),
            pltpu.VMEM((n_node, d), BF16),
            pltpu.VMEM((lent_pad, n_node), BF16),
            pltpu.VMEM((2 * near, d), BF16),
            pltpu.VMEM(far_shape, BF16),
            pltpu.VMEM((2 * near, d), BF16),
            pltpu.VMEM(far_shape, BF16),
            pltpu.VMEM((n_edge, 2 * n_node), BF16),
            pltpu.VMEM((n_edge, ghost_k), BF16),
            pltpu.VMEM((2 * n_node, d), BF16),
            pltpu.VMEM((ghost_k, d), BF16),
            pltpu.VMEM((lent + n_node, n_edge), BF16),
            pltpu.VMEM((n_edge, d), F32),
            pltpu.VMEM((n_edge, d), BF16),
            pltpu.VMEM((2 * near, d), BF16),
            pltpu.VMEM(far_shape, BF16),
            pltpu.VMEM((2 * near, d), BF16),
            pltpu.VMEM(far_shape, BF16),
            pltpu.VMEM((n_node, d), BF16),
            pltpu.VMEM((n_node, d), BF16),
            pltpu.VMEM((n_node, d), F32),
            dma((6,)), dma((blocks,)),
            dma((2,)), dma((2,)), dma((peers,)), dma((peers,)),
            dma((2,)), dma((2,)), dma((peers,)), dma((peers,)),
            dma, dma,
        ],
        compiler_params=pltpu.CompilerParams(
            collective_id=0, has_side_effects=True, vmem_limit_bytes=(48 if peers <= 16 else 60) * 1024 * 1024
        ),
        cost_estimate=pl.CostEstimate(
            flops=2 * macs, bytes_accessed=8 * 1024 * 1024, transcendentals=n_edge * d
        ),
        name="mesh_layer",
    )(
        node_latents, edge_latents, w_edge_in, w_edge_out, w_node_in, w_node_out,
        sender_slot.reshape(1, n_edge), receiver_slot.reshape(1, n_edge), lend, *vectors,
    ))


def solution(mesh):
    nodes = P(("groups", "patch", "sub"), None)
    edges = P(("groups", "patch", "sub", "lane"), None)
    per_edge = P(("groups", "patch", "sub", "lane"))
    lists = P(("groups", "patch", "sub", "lane"), None, None)
    in_specs = (nodes, edges, per_edge, per_edge, lists, lists) + (P(),) * 12
    return jax.shard_map(
        per_device, mesh=mesh, in_specs=in_specs, out_specs=(nodes, edges), check_vma=False
    )
```

```python
import functools

import jax
import jax.numpy as jnp
from jax import lax
from jax.experimental import pallas as pl
from jax.experimental.pallas import tpu as pltpu
from jax.sharding import PartitionSpec as P

MESH = pl.DeviceIdType.MESH
F32 = jnp.float32
BF16 = jnp.bfloat16
LANES = 128
ROW_BLOCK = 256


def mm(a, b):
    return jnp.dot(a, b, preferred_element_type=F32)


def silu(v):
    half = 0.5 * v
    return half + half * jnp.tanh(half)


def norm_rows(values, gain_vec, shift_vec):
    average = jnp.mean(values, axis=-1, keepdims=True)
    centred = values - average
    variance = jnp.mean(centred * centred, axis=-1, keepdims=True)
    return centred * lax.rsqrt(variance + 1e-05) * gain_vec + shift_vec


def ones_where(mask):
    return jnp.where(mask, 1.0, 0.0).astype(BF16)


def iota(shape, dim):
    return lax.broadcasted_iota(jnp.int32, shape, dim)


def layer_kernel(
    dims,
    node_hbm, edge_hbm, wei_hbm, weo_hbm, wni_hbm, wno_hbm,
    snd_hbm, rcv_hbm, near_hbm, far_hbm, *rest,
):
    vec_hbm, rest = rest[:8], rest[8:]
    layer_body(
        dims, (node_hbm, wei_hbm, edge_hbm, weo_hbm, wni_hbm, wno_hbm),
        (snd_hbm, rcv_hbm, near_hbm, far_hbm), vec_hbm, *rest
    )


def layer_body(
    dims, big_hbm, index_hbm, vec_hbm,
    node_out, edge_out,
    snd_ref, rcv_ref, near_idx, far_idx, lend_ref, vecs,
    node_v, edge_v, wei, weo, wni, wno, node_bf,
    lend_sel, near_src, far_src, near_in, far_in,
    pick_own, pick_ghost, proj_own, proj_ghost, drop, pre, msg,
    near_bsrc, far_bsrc, near_back, far_back, lane_src, lane_in, own_sum,
    load_sem, index_sem, vec_sem, store_sem, near_ssem, near_rsem, far_ssem, far_rsem,
    nback_ssem, nback_rsem, fback_ssem, fback_rsem, lane_ssem, lane_rsem,
):
    n_patch, n_sub, n_lane, near, far = dims
    peers = n_patch * n_sub
    far_rows = peers * far
    pack = far * (node_v.shape[1] // LANES)
    n_node, d = node_v.shape
    n_edge = edge_v.shape[0]
    col_parts = d // LANES

    def fetch(sources, targets, sems):
        copies = [
            pltpu.make_async_copy(src, dst, sems.at[i])
            for i, (src, dst) in enumerate(zip(sources, targets))
        ]
        for copy in copies:
            copy.start()
        return copies

    indices = fetch(index_hbm[::-1], (far_idx, near_idx, rcv_ref, snd_ref), index_sem)
    loads = fetch(big_hbm, (node_v, wei, edge_v, weo, wni, wno), load_sem)
    vec_loads = fetch(vec_hbm, [vecs.at[i] for i in range(8)], vec_sem)
    ebi, ebo, egain, eshift, nbi, nbo, ngain, nshift = (vecs.at[i] for i in range(8))

    p = lax.axis_index("patch")
    s = lax.axis_index("sub")
    ln = lax.axis_index("lane")
    g = p * n_sub + s
    nxt = lax.rem(p + 1, n_patch)
    prv = lax.rem(p + n_patch - 1, n_patch)
    other = n_lane - 1 - ln

    def each_peer(fn):
        if peers <= 16:
            for o in range(1, peers):
                fn(o)
        else:
            def body(o, c):
                fn(o)
                return c
            lax.fori_loop(1, peers, body, 0)

    def peer_id(q):
        return {"patch": lax.div(q, n_sub), "sub": lax.rem(q, n_sub)}

    barrier = pltpu.get_barrier_semaphore()

    def greet(o):
        pl.semaphore_signal(
            barrier, inc=1, device_id=peer_id(lax.rem(g + o, peers)), device_id_type=MESH
        )

    each_peer(greet)
    pl.semaphore_signal(barrier, inc=1, device_id={"lane": other}, device_id_type=MESH)

    def column_of(ref, start, width):
        row = ref[:, start:start + width]
        return jnp.transpose(jnp.broadcast_to(row, (LANES, width)))

    lent = 2 * near + far_rows
    indices[0].wait()
    indices[1].wait()
    lend_ref[...] = jnp.zeros(lend_ref.shape, jnp.int32)
    lend_ref[:, :2 * near] = near_idx[...]
    spread = jnp.zeros((peers, far_rows), jnp.int32)
    for k in range(far):
        here = iota((peers, far_rows), 1) == iota((peers, far_rows), 0) * far + k
        spread = jnp.where(here, far_idx[:, k:k + 1], spread)
    lend_ref[:, 2 * near:lent] = jnp.sum(spread, axis=0, keepdims=True)
    for r0 in range(0, lent, LANES):
        col = column_of(lend_ref, r0, LANES)
        for c0 in range(0, n_node, LANES):
            lend_sel[r0:r0 + LANES, c0:c0 + LANES] = ones_where(
                col == iota((LANES, LANES), 1) + c0
            )

    def packer(j):
        r = iota((peers * pack, far_rows), 0)
        c = iota((peers * pack, far_rows), 1)
        return ones_where(r == c // far * pack + j * far + c % far)

    def unpacker(j):
        r = iota((far_rows, peers * pack), 0)
        c = iota((far_rows, peers * pack), 1)
        return ones_where(c == r // far * pack + j * far + r % far)

    def packed(rows):
        total = mm(packer(0), rows[:, :LANES])
        for j in range(1, col_parts):
            total = total + mm(packer(j), rows[:, j * LANES:(j + 1) * LANES])
        return total.astype(BF16)

    def unpacked(block):
        return jnp.concatenate(
            [mm(unpacker(j), block).astype(BF16) for j in range(col_parts)], axis=1
        )

    loads[0].wait()
    node_bf[...] = node_v[...].astype(BF16)
    near_src[...] = mm(lend_sel[:2 * near, :], node_bf[...]).astype(BF16)
    far_src[...] = packed(
        mm(lend_sel[2 * near:lent, :], node_bf[...]).astype(BF16)
    )

    pl.semaphore_wait(barrier, peers)

    def near_copy(i, src, dst, ssem, rsem, patch):
        return pltpu.make_async_remote_copy(
            src_ref=src.at[pl.ds(i * near, near)],
            dst_ref=dst.at[pl.ds(i * near, near)],
            send_sem=ssem.at[i],
            recv_sem=rsem.at[i],
            device_id={"patch": patch},
            device_id_type=MESH,
        )

    def far_copy(o, src, dst, ssem, rsem):
        q = lax.rem(g + o, peers)
        return pltpu.make_async_remote_copy(
            src_ref=src.at[pl.ds(pl.multiple_of(q * pack, pack), pack)],
            dst_ref=dst.at[pl.ds(pl.multiple_of(g * pack, pack), pack)],
            send_sem=ssem.at[o],
            recv_sem=rsem.at[o],
            device_id=peer_id(q),
            device_id_type=MESH,
        )

    def far_arrival(o, src, dst, ssem, rsem):
        q = lax.rem(g + peers - o, peers)
        return pltpu.make_async_remote_copy(
            src_ref=src.at[pl.ds(pl.multiple_of(q * pack, pack), pack)],
            dst_ref=dst.at[pl.ds(pl.multiple_of(q * pack, pack), pack)],
            send_sem=ssem.at[o],
            recv_sem=rsem.at[o],
            device_id=peer_id(q),
            device_id_type=MESH,
        )

    def keep_own(src, dst):
        at = pl.ds(pl.multiple_of(g * pack, pack), pack)
        dst[at, :] = src[at, :]

    ahead = near_copy(0, near_src, near_in, near_ssem, near_rsem, nxt)
    behind = near_copy(1, near_src, near_in, near_ssem, near_rsem, prv)
    each_peer(lambda o: far_copy(o, far_src, far_in, far_ssem, far_rsem).start())
    ahead.start()
    behind.start()
    keep_own(far_src, far_in)

    indices[2].wait()
    indices[3].wait()
    for load in vec_loads:
        load.wait()

    loads[1].wait()
    proj_own[:n_node, :] = mm(node_bf[...], wei[d:2 * d, :]).astype(BF16)
    proj_own[n_node:, :] = mm(node_bf[...], wei[2 * d:, :]).astype(BF16)
    first_near = n_node
    first_far = n_node + 2 * near
    far_cols = proj_ghost.shape[0] - 4 * near
    for e0 in range(0, n_edge, LANES):
        scol = column_of(snd_ref, e0, LANES)
        rcol = column_of(rcv_ref, e0, LANES)
        rows = slice(e0, e0 + LANES)
        lane_ids = iota((LANES, LANES), 1)
        for c0 in range(0, n_node, LANES):
            pick_own[rows, c0:c0 + LANES] = ones_where(scol == lane_ids + c0)
            pick_own[rows, n_node + c0:n_node + c0 + LANES] = ones_where(rcol == lane_ids + c0)
        for c0 in range(0, 2 * near, LANES):
            at = first_near + c0
            pick_ghost[rows, c0:c0 + LANES] = ones_where(scol == lane_ids + at)
            pick_ghost[rows, 2 * near + c0:2 * near + c0 + LANES] = ones_where(rcol == lane_ids + at)
        for c0 in range(0, far_cols, LANES):
            c = lane_ids + c0
            is_s = c < far_rows
            slot = jnp.where(is_s, scol, rcol)
            name = jnp.where(is_s, c, c - far_rows) + first_far
            pick_ghost[rows, 4 * near + c0:4 * near + c0 + LANES] = ones_where(slot == name)

    loads[2].wait()
    for e0 in range(0, n_edge, ROW_BLOCK):
        rows = slice(e0, e0 + ROW_BLOCK)
        pre[rows, :] = mm(edge_v[rows, :], wei[:d, :]) + mm(pick_own[rows, :], proj_own[...]) + ebi[...]

    rcv_row = rcv_ref[...]
    for r0, base, count in (
        (0, first_near, 2 * near), (2 * near, first_far, far_rows), (lent, 0, n_node)
    ):
        drop[r0:r0 + count, :] = ones_where(iota((count, n_edge), 0) + base == rcv_row)
    if far_cols > 2 * far_rows:
        proj_ghost[4 * near + 2 * far_rows:, :] = jnp.zeros((far_cols - 2 * far_rows, d), BF16)

    each_peer(lambda o: far_arrival(o, far_src, far_in, far_ssem, far_rsem).wait_recv())
    far_nodes = unpacked(far_in[...])
    proj_ghost[4 * near:4 * near + far_rows, :] = mm(far_nodes, wei[d:2 * d, :]).astype(BF16)
    proj_ghost[4 * near + far_rows:4 * near + 2 * far_rows, :] = mm(
        far_nodes, wei[2 * d:, :]
    ).astype(BF16)
    ahead.wait_recv()
    behind.wait_recv()
    proj_ghost[:2 * near, :] = mm(near_in[...], wei[d:2 * d, :]).astype(BF16)
    proj_ghost[2 * near:4 * near, :] = mm(near_in[...], wei[2 * d:, :]).astype(BF16)

    loads[3].wait()
    stores = []
    for i, e0 in enumerate(range(0, n_edge, ROW_BLOCK)):
        rows = slice(e0, e0 + ROW_BLOCK)
        hidden = silu(pre[rows, :] + mm(pick_ghost[rows, :], proj_ghost[...])).astype(BF16)
        message = norm_rows(mm(hidden, weo[...]) + ebo[...], egain[...], eshift[...])
        msg[rows, :] = message.astype(BF16)
        edge_v[rows, :] = (edge_v[rows, :].astype(F32) + message).astype(BF16)
        store = pltpu.make_async_copy(edge_v.at[rows], edge_out.at[rows], store_sem.at[i])
        store.start()
        stores.append(store)

    near_bsrc[...] = mm(drop[:2 * near, :], msg[...]).astype(BF16)
    back_prev = near_copy(0, near_bsrc, near_back, nback_ssem, nback_rsem, prv)
    back_next = near_copy(1, near_bsrc, near_back, nback_ssem, nback_rsem, nxt)
    back_prev.start()
    back_next.start()
    far_bsrc[...] = packed(mm(drop[2 * near:lent, :], msg[...]).astype(BF16))
    each_peer(lambda o: far_copy(o, far_bsrc, far_back, fback_ssem, fback_rsem).start())
    keep_own(far_bsrc, far_back)
    own_sum[...] = mm(drop[lent:, :], msg[...])

    loads[4].wait()
    loads[5].wait()
    node_pre = mm(node_bf[...], wni[:d, :]) + nbi[...]
    give = ones_where(iota((n_node, lent), 0) == lend_ref[:, :lent])

    each_peer(lambda o: far_arrival(o, far_bsrc, far_back, fback_ssem, fback_rsem).wait_recv())
    own_sum[...] += mm(give[:, 2 * near:], unpacked(far_back[...]))
    back_prev.wait_recv()
    back_next.wait_recv()
    lane_src[...] = (own_sum[...] + mm(give[:, :2 * near], near_back[...])).astype(BF16)
    swap = pltpu.make_async_remote_copy(
        src_ref=lane_src, dst_ref=lane_in, send_sem=lane_ssem, recv_sem=lane_rsem,
        device_id={"lane": other}, device_id_type=MESH,
    )
    swap.start()
    swap.wait_recv()
    summed = (lane_src[...].astype(F32) + lane_in[...].astype(F32)).astype(BF16)
    node_hidden = silu(node_pre + mm(summed, wni[d:, :])).astype(BF16)
    node_out[...] = node_v[...] + norm_rows(
        mm(node_hidden, wno[...]) + nbo[...], ngain[...], nshift[...]
    )

    ahead.wait_send()
    behind.wait_send()
    back_prev.wait_send()
    back_next.wait_send()
    swap.wait_send()
    each_peer(lambda o: far_copy(o, far_src, far_in, far_ssem, far_rsem).wait_send())
    each_peer(lambda o: far_copy(o, far_bsrc, far_back, fback_ssem, fback_rsem).wait_send())
    for store in stores:
        store.wait()


def per_device(
    node_latents, edge_latents, sender_slot, receiver_slot, near_send, far_send,
    w_edge_in, w_edge_out, w_node_in, w_node_out,
    edge_bias_in, edge_bias_out, edge_gain, edge_shift,
    node_bias_in, node_bias_out, node_gain, node_shift,
):
    n_node, d = node_latents.shape
    n_edge = edge_latents.shape[0]
    near = near_send.shape[2]
    peers, far = far_send.shape[1:]
    n_patch, n_sub, n_lane = (lax.axis_size(a) for a in ("patch", "sub", "lane"))
    far_rows = peers * far
    lent = 2 * near + far_rows
    lent_pad = -(-lent // LANES) * LANES
    ghost_k = 4 * near + -(-2 * far_rows // LANES) * LANES
    pack = far * (d // LANES)
    blocks = n_edge // ROW_BLOCK
    vectors = [v.reshape(1, d) for v in (
        edge_bias_in, edge_bias_out, edge_gain, edge_shift,
        node_bias_in, node_bias_out, node_gain, node_shift)]
    hbm = pl.BlockSpec(memory_space=pltpu.HBM)
    vmem = pl.BlockSpec(memory_space=pltpu.VMEM)
    dma = pltpu.SemaphoreType.DMA
    far_shape = (peers * pack, LANES)
    macs = n_edge * d * (3 * d + ghost_k + lent + n_node) + n_node * d * 6 * d
    return tuple(pl.pallas_call(
        functools.partial(layer_kernel, (n_patch, n_sub, n_lane, near, far)),
        out_shape=(
            jax.ShapeDtypeStruct((n_node, d), F32),
            jax.ShapeDtypeStruct((n_edge, d), BF16),
        ),
        in_specs=[hbm] * (10 + len(vectors)),
        out_specs=(vmem, hbm),
        scratch_shapes=[
            pltpu.VMEM((1, n_edge), jnp.int32),
            pltpu.VMEM((1, n_edge), jnp.int32),
            pltpu.VMEM((1, 2 * near), jnp.int32),
            pltpu.VMEM((peers, far), jnp.int32),
            pltpu.VMEM((1, lent_pad), jnp.int32),
            pltpu.VMEM((len(vectors), 1, d), F32),
            pltpu.VMEM((n_node, d), F32),
            pltpu.VMEM((n_edge, d), BF16),
            pltpu.VMEM(w_edge_in.shape, BF16),
            pltpu.VMEM(w_edge_out.shape, BF16),
            pltpu.VMEM(w_node_in.shape, BF16),
            pltpu.VMEM(w_node_out.shape, BF16),
            pltpu.VMEM((n_node, d), BF16),
            pltpu.VMEM((lent_pad, n_node), BF16),
            pltpu.VMEM((2 * near, d), BF16),
            pltpu.VMEM(far_shape, BF16),
            pltpu.VMEM((2 * near, d), BF16),
            pltpu.VMEM(far_shape, BF16),
            pltpu.VMEM((n_edge, 2 * n_node), BF16),
            pltpu.VMEM((n_edge, ghost_k), BF16),
            pltpu.VMEM((2 * n_node, d), BF16),
            pltpu.VMEM((ghost_k, d), BF16),
            pltpu.VMEM((lent + n_node, n_edge), BF16),
            pltpu.VMEM((n_edge, d), F32),
            pltpu.VMEM((n_edge, d), BF16),
            pltpu.VMEM((2 * near, d), BF16),
            pltpu.VMEM(far_shape, BF16),
            pltpu.VMEM((2 * near, d), BF16),
            pltpu.VMEM(far_shape, BF16),
            pltpu.VMEM((n_node, d), BF16),
            pltpu.VMEM((n_node, d), BF16),
            pltpu.VMEM((n_node, d), F32),
            dma((6,)), dma((4,)), dma((len(vectors),)), dma((blocks,)),
            dma((2,)), dma((2,)), dma((peers,)), dma((peers,)),
            dma((2,)), dma((2,)), dma((peers,)), dma((peers,)),
            dma, dma,
        ],
        compiler_params=pltpu.CompilerParams(
            collective_id=0, has_side_effects=True, vmem_limit_bytes=62 * 1024 * 1024
        ),
        cost_estimate=pl.CostEstimate(
            flops=2 * macs, bytes_accessed=8 * 1024 * 1024, transcendentals=n_edge * d
        ),
        name="mesh_layer",
    )(
        node_latents, edge_latents, w_edge_in, w_edge_out, w_node_in, w_node_out,
        sender_slot.reshape(1, n_edge), receiver_slot.reshape(1, n_edge),
        near_send.reshape(1, 2 * near), far_send.reshape(peers, far), *vectors,
    ))


def solution(mesh):
    nodes = P(("groups", "patch", "sub"), None)
    edges = P(("groups", "patch", "sub", "lane"), None)
    per_edge = P(("groups", "patch", "sub", "lane"))
    lists = P(("groups", "patch", "sub", "lane"), None, None)
    in_specs = (nodes, edges, per_edge, per_edge, lists, lists) + (P(),) * 12
    return jax.shard_map(
        per_device, mesh=mesh, in_specs=in_specs, out_specs=(nodes, edges), check_vma=False
    )
```

```python
import functools

import jax
import jax.numpy as jnp
from jax import lax
from jax.experimental import pallas as pl
from jax.experimental.pallas import tpu as pltpu
from jax.sharding import PartitionSpec as P

MESH = pl.DeviceIdType.MESH
F32 = jnp.float32
BF16 = jnp.bfloat16
LANES = 128
ROW_BLOCK = 256
PIECES = 4


def mm(a, b):
    return jnp.dot(a, b, preferred_element_type=F32)


def silu(v):
    half = 0.5 * v
    return half + half * jnp.tanh(half)


def norm_rows(values, gain_vec, shift_vec):
    average = jnp.mean(values, axis=-1, keepdims=True)
    centred = values - average
    variance = jnp.mean(centred * centred, axis=-1, keepdims=True)
    return centred * lax.rsqrt(variance + 1e-05) * gain_vec + shift_vec


def ones_where(mask):
    return jnp.where(mask, 1.0, 0.0).astype(BF16)


def iota(shape, dim):
    return lax.broadcasted_iota(jnp.int32, shape, dim)


def layer_kernel(
    dims,
    node_hbm, edge_hbm, wei_hbm, weo_hbm, wni_hbm, wno_hbm,
    snd_hbm, rcv_hbm, near_hbm, far_hbm, *rest,
):
    vec_hbm, rest = rest[:8], rest[8:]
    layer_body(
        dims, (node_hbm, wei_hbm, edge_hbm, weo_hbm, wni_hbm, wno_hbm),
        (snd_hbm, rcv_hbm, near_hbm, far_hbm), vec_hbm, *rest
    )


def layer_body(
    dims, big_hbm, index_hbm, vec_hbm,
    node_out, edge_out,
    snd_ref, rcv_ref, near_idx, far_idx, lend_ref, vecs,
    node_v, edge_v, wei, weo, wni, wno, node_bf,
    lend_sel, near_src, far_src, near_in, far_in,
    pick_own, pick_ghost, proj_own, proj_ghost, drop, pre, msg,
    near_bsrc, far_bsrc, near_back, far_back, lane_src, lane_in, own_sum,
    load_sem, index_sem, vec_sem, store_sem, near_ssem, near_rsem, far_ssem, far_rsem,
    nback_ssem, nback_rsem, fback_ssem, fback_rsem, lane_ssem, lane_rsem,
):
    n_patch, n_sub, n_lane, near, far = dims
    peers = n_patch * n_sub
    far_rows = peers * far
    pack = far * (node_v.shape[1] // LANES)
    n_node, d = node_v.shape
    n_edge = edge_v.shape[0]
    col_parts = d // LANES

    def fetch(sources, targets, sems):
        copies = [
            pltpu.make_async_copy(src, dst, sems.at[i])
            for i, (src, dst) in enumerate(zip(sources, targets))
        ]
        for copy in copies:
            copy.start()
        return copies

    indices = fetch(index_hbm[::-1], (far_idx, near_idx, rcv_ref, snd_ref), index_sem)
    loads = fetch(big_hbm, (node_v, wei, edge_v, weo, wni, wno), load_sem)
    vec_loads = fetch(vec_hbm, [vecs.at[i] for i in range(8)], vec_sem)
    ebi, ebo, egain, eshift, nbi, nbo, ngain, nshift = (vecs.at[i] for i in range(8))

    p = lax.axis_index("patch")
    s = lax.axis_index("sub")
    ln = lax.axis_index("lane")
    g = p * n_sub + s
    nxt = lax.rem(p + 1, n_patch)
    prv = lax.rem(p + n_patch - 1, n_patch)
    other = n_lane - 1 - ln

    def each_peer(fn):
        if peers <= 16:
            for o in range(1, peers):
                fn(o)
        else:
            def body(o, c):
                fn(o)
                return c
            lax.fori_loop(1, peers, body, 0)

    def peer_id(q):
        return {"patch": lax.div(q, n_sub), "sub": lax.rem(q, n_sub)}

    barrier = pltpu.get_barrier_semaphore()

    def greet(o):
        pl.semaphore_signal(
            barrier, inc=1, device_id=peer_id(lax.rem(g + o, peers)), device_id_type=MESH
        )

    each_peer(greet)
    pl.semaphore_signal(barrier, inc=1, device_id={"lane": other}, device_id_type=MESH)

    def column_of(ref, start, width):
        row = ref[:, start:start + width]
        return jnp.transpose(jnp.broadcast_to(row, (LANES, width)))

    lent = 2 * near + far_rows
    indices[0].wait()
    indices[1].wait()
    lend_ref[...] = jnp.zeros(lend_ref.shape, jnp.int32)
    lend_ref[:, :2 * near] = near_idx[...]
    for k in range(far):
        at = 2 * near + k * peers
        lend_ref[:, at:at + peers] = far_idx[k:k + 1, :]
    for r0 in range(0, lent, LANES):
        col = column_of(lend_ref, r0, LANES)
        for c0 in range(0, n_node, LANES):
            lend_sel[r0:r0 + LANES, c0:c0 + LANES] = ones_where(
                col == iota((LANES, LANES), 1) + c0
            )

    def packer(j):
        r = iota((peers * pack, far_rows), 0)
        c = iota((peers * pack, far_rows), 1)
        return ones_where(r == c % peers * pack + j * far + c // peers)

    def unpacker(j):
        r = iota((far_rows, peers * pack), 0)
        c = iota((far_rows, peers * pack), 1)
        return ones_where(c == r % peers * pack + j * far + r // peers)

    def packed(rows):
        total = mm(packer(0), rows[:, :LANES])
        for j in range(1, col_parts):
            total = total + mm(packer(j), rows[:, j * LANES:(j + 1) * LANES])
        return total.astype(BF16)

    def unpacked(block):
        return jnp.concatenate(
            [mm(unpacker(j), block).astype(BF16) for j in range(col_parts)], axis=1
        )

    loads[0].wait()
    node_bf[...] = node_v[...].astype(BF16)
    near_src[...] = mm(lend_sel[:2 * near, :], node_bf[...]).astype(BF16)

    pl.semaphore_wait(barrier, peers)

    def near_copy(i, src, dst, ssem, rsem, patch):
        return pltpu.make_async_remote_copy(
            src_ref=src.at[pl.ds(i * near, near)],
            dst_ref=dst.at[pl.ds(i * near, near)],
            send_sem=ssem.at[i],
            recv_sem=rsem.at[i],
            device_id={"patch": patch},
            device_id_type=MESH,
        )

    def far_copy(o, src, dst, ssem, rsem):
        q = lax.rem(g + o, peers)
        return pltpu.make_async_remote_copy(
            src_ref=src.at[pl.ds(pl.multiple_of(q * pack, pack), pack)],
            dst_ref=dst.at[pl.ds(pl.multiple_of(g * pack, pack), pack)],
            send_sem=ssem.at[o],
            recv_sem=rsem.at[o],
            device_id=peer_id(q),
            device_id_type=MESH,
        )

    def far_arrival(o, src, dst, ssem, rsem):
        q = lax.rem(g + peers - o, peers)
        return pltpu.make_async_remote_copy(
            src_ref=src.at[pl.ds(pl.multiple_of(q * pack, pack), pack)],
            dst_ref=dst.at[pl.ds(pl.multiple_of(q * pack, pack), pack)],
            send_sem=ssem.at[o],
            recv_sem=rsem.at[o],
            device_id=peer_id(q),
            device_id_type=MESH,
        )

    def keep_own(src, dst):
        at = pl.ds(pl.multiple_of(g * pack, pack), pack)
        dst[at, :] = src[at, :]

    ahead = near_copy(0, near_src, near_in, near_ssem, near_rsem, nxt)
    behind = near_copy(1, near_src, near_in, near_ssem, near_rsem, prv)
    ahead.start()
    behind.start()
    far_src[...] = packed(
        mm(lend_sel[2 * near:lent, :], node_bf[...]).astype(BF16)
    )
    each_peer(lambda o: far_copy(o, far_src, far_in, far_ssem, far_rsem).start())
    keep_own(far_src, far_in)

    indices[2].wait()
    indices[3].wait()
    for load in vec_loads:
        load.wait()

    loads[1].wait()
    proj_own[:n_node, :] = mm(node_bf[...], wei[d:2 * d, :]).astype(BF16)
    proj_own[n_node:, :] = mm(node_bf[...], wei[2 * d:, :]).astype(BF16)
    first_near = n_node
    first_far = n_node + 2 * near
    far_cols = proj_ghost.shape[0] - 4 * near
    for e0 in range(0, n_edge, LANES):
        scol = column_of(snd_ref, e0, LANES)
        rcol = column_of(rcv_ref, e0, LANES)
        rows = slice(e0, e0 + LANES)
        lane_ids = iota((LANES, LANES), 1)
        for c0 in range(0, n_node, LANES):
            pick_own[rows, c0:c0 + LANES] = ones_where(scol == lane_ids + c0)
            pick_own[rows, n_node + c0:n_node + c0 + LANES] = ones_where(rcol == lane_ids + c0)
        for c0 in range(0, 2 * near, LANES):
            at = first_near + c0
            pick_ghost[rows, c0:c0 + LANES] = ones_where(scol == lane_ids + at)
            pick_ghost[rows, 2 * near + c0:2 * near + c0 + LANES] = ones_where(rcol == lane_ids + at)
        for c0 in range(0, far_cols, LANES):
            c = lane_ids + c0
            is_s = c < far_rows
            slot = jnp.where(is_s, scol, rcol)
            row = jnp.where(is_s, c, c - far_rows)
            name = first_far + row % peers * far + row // peers
            pick_ghost[rows, 4 * near + c0:4 * near + c0 + LANES] = ones_where(slot == name)

    loads[2].wait()
    for e0 in range(0, n_edge, ROW_BLOCK):
        rows = slice(e0, e0 + ROW_BLOCK)
        pre[rows, :] = mm(edge_v[rows, :], wei[:d, :]) + mm(pick_own[rows, :], proj_own[...]) + ebi[...]

    rcv_row = rcv_ref[...]
    for r0, base, count in ((0, first_near, 2 * near), (lent, 0, n_node)):
        drop[r0:r0 + count, :] = ones_where(iota((count, n_edge), 0) + base == rcv_row)
    row = iota((far_rows, n_edge), 0)
    drop[2 * near:lent, :] = ones_where(first_far + row % peers * far + row // peers == rcv_row)
    if far_cols > 2 * far_rows:
        proj_ghost[4 * near + 2 * far_rows:, :] = jnp.zeros((far_cols - 2 * far_rows, d), BF16)

    each_peer(lambda o: far_arrival(o, far_src, far_in, far_ssem, far_rsem).wait_recv())
    far_nodes = unpacked(far_in[...])
    proj_ghost[4 * near:4 * near + far_rows, :] = mm(far_nodes, wei[d:2 * d, :]).astype(BF16)
    proj_ghost[4 * near + far_rows:4 * near + 2 * far_rows, :] = mm(
        far_nodes, wei[2 * d:, :]
    ).astype(BF16)
    ahead.wait_recv()
    behind.wait_recv()
    proj_ghost[:2 * near, :] = mm(near_in[...], wei[d:2 * d, :]).astype(BF16)
    proj_ghost[2 * near:4 * near, :] = mm(near_in[...], wei[2 * d:, :]).astype(BF16)

    loads[3].wait()
    stores = []
    for i, e0 in enumerate(range(0, n_edge, ROW_BLOCK)):
        rows = slice(e0, e0 + ROW_BLOCK)
        hidden = silu(pre[rows, :] + mm(pick_ghost[rows, :], proj_ghost[...])).astype(BF16)
        message = norm_rows(mm(hidden, weo[...]) + ebo[...], egain[...], eshift[...])
        msg[rows, :] = message.astype(BF16)
        edge_v[rows, :] = (edge_v[rows, :].astype(F32) + message).astype(BF16)
        store = pltpu.make_async_copy(edge_v.at[rows], edge_out.at[rows], store_sem.at[i])
        store.start()
        stores.append(store)

    near_bsrc[...] = mm(drop[:2 * near, :], msg[...]).astype(BF16)
    back_prev = near_copy(0, near_bsrc, near_back, nback_ssem, nback_rsem, prv)
    back_next = near_copy(1, near_bsrc, near_back, nback_ssem, nback_rsem, nxt)
    back_prev.start()
    back_next.start()
    far_bsrc[...] = packed(mm(drop[2 * near:lent, :], msg[...]).astype(BF16))
    each_peer(lambda o: far_copy(o, far_bsrc, far_back, fback_ssem, fback_rsem).start())
    keep_own(far_bsrc, far_back)
    own_sum[...] = mm(drop[lent:, :], msg[...])

    loads[4].wait()
    loads[5].wait()
    node_pre = mm(node_bf[...], wni[:d, :]) + nbi[...]
    give = ones_where(iota((n_node, lent), 0) == lend_ref[:, :lent])

    each_peer(lambda o: far_arrival(o, far_bsrc, far_back, fback_ssem, fback_rsem).wait_recv())
    own_sum[...] += mm(give[:, 2 * near:], unpacked(far_back[...]))
    back_prev.wait_recv()
    back_next.wait_recv()
    lane_src[...] = (own_sum[...] + mm(give[:, :2 * near], near_back[...])).astype(BF16)
    swap = pltpu.make_async_remote_copy(
        src_ref=lane_src, dst_ref=lane_in, send_sem=lane_ssem, recv_sem=lane_rsem,
        device_id={"lane": other}, device_id_type=MESH,
    )
    swap.start()
    swap.wait_recv()
    summed = (lane_src[...].astype(F32) + lane_in[...].astype(F32)).astype(BF16)
    node_hidden = silu(node_pre + mm(summed, wni[d:, :])).astype(BF16)
    node_out[...] = node_v[...] + norm_rows(
        mm(node_hidden, wno[...]) + nbo[...], ngain[...], nshift[...]
    )

    ahead.wait_send()
    behind.wait_send()
    back_prev.wait_send()
    back_next.wait_send()
    swap.wait_send()
    each_peer(lambda o: far_copy(o, far_src, far_in, far_ssem, far_rsem).wait_send())
    each_peer(lambda o: far_copy(o, far_bsrc, far_back, fback_ssem, fback_rsem).wait_send())
    for store in stores:
        store.wait()


def hand_over(node_in, edge_in, node_out, edge_out, sems):
    copies = []
    for a, (src, dst) in enumerate(((edge_in, edge_out), (node_in, node_out))):
        step = src.shape[0] // PIECES
        for i in range(PIECES):
            rows = pl.ds(i * step, step)
            copies.append(pltpu.make_async_copy(
                src.at[rows], dst.at[rows], sems.at[a * PIECES + i]
            ))
    for copy in copies:
        copy.start()
    for copy in copies:
        copy.wait()


def per_device(
    node_latents, edge_latents, sender_slot, receiver_slot, near_send, far_send,
    w_edge_in, w_edge_out, w_node_in, w_node_out,
    edge_bias_in, edge_bias_out, edge_gain, edge_shift,
    node_bias_in, node_bias_out, node_gain, node_shift,
):
    n_node, d = node_latents.shape
    n_edge = edge_latents.shape[0]
    near = near_send.shape[2]
    peers, far = far_send.shape[1:]
    n_patch, n_sub, n_lane = (lax.axis_size(a) for a in ("patch", "sub", "lane"))
    far_rows = peers * far
    lent = 2 * near + far_rows
    lent_pad = -(-lent // LANES) * LANES
    ghost_k = 4 * near + -(-2 * far_rows // LANES) * LANES
    pack = far * (d // LANES)
    blocks = n_edge // ROW_BLOCK
    vectors = [v.reshape(1, d) for v in (
        edge_bias_in, edge_bias_out, edge_gain, edge_shift,
        node_bias_in, node_bias_out, node_gain, node_shift)]
    hbm = pl.BlockSpec(memory_space=pltpu.HBM)
    vmem = pl.BlockSpec(memory_space=pltpu.VMEM)
    dma = pltpu.SemaphoreType.DMA
    far_shape = (peers * pack, LANES)
    macs = n_edge * d * (3 * d + ghost_k + lent + n_node) + n_node * d * 6 * d
    results = pl.pallas_call(
        functools.partial(layer_kernel, (n_patch, n_sub, n_lane, near, far)),
        out_shape=(
            jax.ShapeDtypeStruct((n_node, d), F32),
            jax.ShapeDtypeStruct((n_edge, d), BF16),
        ),
        in_specs=[hbm] * (10 + len(vectors)),
        out_specs=(vmem, hbm),
        scratch_shapes=[
            pltpu.VMEM((1, n_edge), jnp.int32),
            pltpu.VMEM((1, n_edge), jnp.int32),
            pltpu.VMEM((1, 2 * near), jnp.int32),
            pltpu.VMEM((far, peers), jnp.int32),
            pltpu.VMEM((1, lent_pad), jnp.int32),
            pltpu.VMEM((len(vectors), 1, d), F32),
            pltpu.VMEM((n_node, d), F32),
            pltpu.VMEM((n_edge, d), BF16),
            pltpu.VMEM(w_edge_in.shape, BF16),
            pltpu.VMEM(w_edge_out.shape, BF16),
            pltpu.VMEM(w_node_in.shape, BF16),
            pltpu.VMEM(w_node_out.shape, BF16),
            pltpu.VMEM((n_node, d), BF16),
            pltpu.VMEM((lent_pad, n_node), BF16),
            pltpu.VMEM((2 * near, d), BF16),
            pltpu.VMEM(far_shape, BF16),
            pltpu.VMEM((2 * near, d), BF16),
            pltpu.VMEM(far_shape, BF16),
            pltpu.VMEM((n_edge, 2 * n_node), BF16),
            pltpu.VMEM((n_edge, ghost_k), BF16),
            pltpu.VMEM((2 * n_node, d), BF16),
            pltpu.VMEM((ghost_k, d), BF16),
            pltpu.VMEM((lent + n_node, n_edge), BF16),
            pltpu.VMEM((n_edge, d), F32),
            pltpu.VMEM((n_edge, d), BF16),
            pltpu.VMEM((2 * near, d), BF16),
            pltpu.VMEM(far_shape, BF16),
            pltpu.VMEM((2 * near, d), BF16),
            pltpu.VMEM(far_shape, BF16),
            pltpu.VMEM((n_node, d), BF16),
            pltpu.VMEM((n_node, d), BF16),
            pltpu.VMEM((n_node, d), F32),
            dma((6,)), dma((4,)), dma((len(vectors),)), dma((blocks,)),
            dma((2,)), dma((2,)), dma((peers,)), dma((peers,)),
            dma((2,)), dma((2,)), dma((peers,)), dma((peers,)),
            dma, dma,
        ],
        compiler_params=pltpu.CompilerParams(
            collective_id=0, has_side_effects=True, vmem_limit_bytes=62 * 1024 * 1024
        ),
        cost_estimate=pl.CostEstimate(
            flops=2 * macs, bytes_accessed=8 * 1024 * 1024, transcendentals=n_edge * d
        ),
        name="mesh_layer",
    )(
        node_latents, edge_latents, w_edge_in, w_edge_out, w_node_in, w_node_out,
        sender_slot.reshape(1, n_edge), receiver_slot.reshape(1, n_edge),
        near_send.reshape(1, 2 * near), jnp.swapaxes(far_send, 1, 2).reshape(far, peers), *vectors,
    )
    return tuple(pl.pallas_call(
        hand_over,
        out_shape=tuple(jax.ShapeDtypeStruct(r.shape, r.dtype) for r in results),
        in_specs=[hbm] * 2,
        out_specs=(hbm, hbm),
        scratch_shapes=[dma((2 * PIECES,))],
        compiler_params=pltpu.CompilerParams(vmem_limit_bytes=62 * 1024 * 1024),
        name="hand_over",
    )(*results))


def solution(mesh):
    nodes = P(("groups", "patch", "sub"), None)
    edges = P(("groups", "patch", "sub", "lane"), None)
    per_edge = P(("groups", "patch", "sub", "lane"))
    lists = P(("groups", "patch", "sub", "lane"), None, None)
    in_specs = (nodes, edges, per_edge, per_edge, lists, lists) + (P(),) * 12
    return jax.shard_map(
        per_device, mesh=mesh, in_specs=in_specs, out_specs=(nodes, edges), check_vma=False
    )
```

```python
import functools

import jax
import jax.numpy as jnp
from jax import lax
from jax.experimental import pallas as pl
from jax.experimental.pallas import tpu as pltpu
from jax.sharding import PartitionSpec as P

MESH = pl.DeviceIdType.MESH
F32 = jnp.float32
BF16 = jnp.bfloat16
LANES = 128
ROW_BLOCK = 256
PIECES = 4


def mm(a, b):
    return jnp.dot(a, b, preferred_element_type=F32)


def silu(v):
    half = 0.5 * v
    return half + half * jnp.tanh(half)


def norm_rows(values, gain_vec, shift_vec):
    average = jnp.mean(values, axis=-1, keepdims=True)
    centred = values - average
    variance = jnp.mean(centred * centred, axis=-1, keepdims=True)
    return centred * lax.rsqrt(variance + 1e-05) * gain_vec + shift_vec


def ones_where(mask):
    return jnp.where(mask, 1.0, 0.0).astype(BF16)


def iota(shape, dim):
    return lax.broadcasted_iota(jnp.int32, shape, dim)


def layer_kernel(
    dims,
    node_hbm, edge_hbm, wei_hbm, weo_hbm, wni_hbm, wno_hbm,
    snd_hbm, rcv_hbm, near_hbm, far_hbm, *rest,
):
    vec_hbm, rest = rest[:8], rest[8:]
    layer_body(
        dims, (node_hbm, wei_hbm, edge_hbm, weo_hbm, wni_hbm, wno_hbm),
        (snd_hbm, rcv_hbm, near_hbm, far_hbm), vec_hbm, *rest
    )


def layer_body(
    dims, big_hbm, index_hbm, vec_hbm,
    node_out, edge_out,
    snd_ref, rcv_ref, near_idx, far_idx, lend_ref, vecs,
    node_v, edge_v, wei, weo, wni, wno, node_bf,
    lend_sel, near_src, far_src, near_in, far_in,
    pick_own, pick_ghost, proj_own, proj_ghost, drop, pre, msg,
    near_bsrc, far_bsrc, near_back, far_back, lane_src, lane_in, own_sum,
    load_sem, index_sem, vec_sem, store_sem, near_ssem, near_rsem, far_ssem, far_rsem,
    nback_ssem, nback_rsem, fback_ssem, fback_rsem, lane_ssem, lane_rsem,
):
    n_patch, n_sub, n_lane, near, far = dims
    peers = n_patch * n_sub
    far_rows = peers * far
    pack = far * (node_v.shape[1] // LANES)
    n_node, d = node_v.shape
    n_edge = edge_v.shape[0]
    col_parts = d // LANES

    def fetch(sources, targets, sems):
        copies = [
            pltpu.make_async_copy(src, dst, sems.at[i])
            for i, (src, dst) in enumerate(zip(sources, targets))
        ]
        for copy in copies:
            copy.start()
        return copies

    indices = fetch(index_hbm[::-1], (far_idx, near_idx, rcv_ref, snd_ref), index_sem)
    loads = fetch(big_hbm, (node_v, wei, edge_v, weo, wni, wno), load_sem)
    vec_loads = fetch(vec_hbm, [vecs.at[i] for i in range(8)], vec_sem)
    ebi, ebo, egain, eshift, nbi, nbo, ngain, nshift = (vecs.at[i] for i in range(8))

    p = lax.axis_index("patch")
    s = lax.axis_index("sub")
    ln = lax.axis_index("lane")
    g = p * n_sub + s
    nxt = lax.rem(p + 1, n_patch)
    prv = lax.rem(p + n_patch - 1, n_patch)
    other = n_lane - 1 - ln

    def each_peer(fn):
        if peers <= 16:
            for o in range(1, peers):
                fn(o)
        else:
            def body(o, c):
                fn(o)
                return c
            lax.fori_loop(1, peers, body, 0)

    def peer_id(q):
        return {"patch": lax.div(q, n_sub), "sub": lax.rem(q, n_sub)}

    barrier = pltpu.get_barrier_semaphore()

    def greet(o):
        pl.semaphore_signal(
            barrier, inc=1, device_id=peer_id(lax.rem(g + o, peers)), device_id_type=MESH
        )

    each_peer(greet)
    pl.semaphore_signal(barrier, inc=1, device_id={"lane": other}, device_id_type=MESH)

    def column_of(ref, start, width):
        row = ref[:, start:start + width]
        return jnp.transpose(jnp.broadcast_to(row, (LANES, width)))

    lent = 2 * near + far_rows
    indices[0].wait()
    indices[1].wait()
    lend_ref[...] = jnp.zeros(lend_ref.shape, jnp.int32)
    lend_ref[:, :2 * near] = near_idx[...]
    for k in range(far):
        at = 2 * near + k * peers
        lend_ref[:, at:at + peers] = far_idx[k:k + 1, :]
    for r0 in range(0, lent, LANES):
        col = column_of(lend_ref, r0, LANES)
        for c0 in range(0, n_node, LANES):
            lend_sel[r0:r0 + LANES, c0:c0 + LANES] = ones_where(
                col == iota((LANES, LANES), 1) + c0
            )

    def packer(j):
        r = iota((peers * pack, far_rows), 0)
        c = iota((peers * pack, far_rows), 1)
        return ones_where(r == c % peers * pack + j * far + c // peers)

    def unpacker(j):
        r = iota((far_rows, peers * pack), 0)
        c = iota((far_rows, peers * pack), 1)
        return ones_where(c == r % peers * pack + j * far + r // peers)

    def packed(rows):
        total = mm(packer(0), rows[:, :LANES])
        for j in range(1, col_parts):
            total = total + mm(packer(j), rows[:, j * LANES:(j + 1) * LANES])
        return total.astype(BF16)

    def unpacked(block):
        return jnp.concatenate(
            [mm(unpacker(j), block).astype(BF16) for j in range(col_parts)], axis=1
        )

    loads[0].wait()
    node_bf[...] = node_v[...].astype(BF16)
    near_src[...] = mm(lend_sel[:2 * near, :], node_bf[...]).astype(BF16)

    far_src[...] = packed(
        mm(lend_sel[2 * near:lent, :], node_bf[...]).astype(BF16)
    )
    pl.semaphore_wait(barrier, peers)

    def near_copy(i, src, dst, ssem, rsem, patch):
        return pltpu.make_async_remote_copy(
            src_ref=src.at[pl.ds(i * near, near)],
            dst_ref=dst.at[pl.ds(i * near, near)],
            send_sem=ssem.at[i],
            recv_sem=rsem.at[i],
            device_id={"patch": patch},
            device_id_type=MESH,
        )

    def far_copy(o, src, dst, ssem, rsem):
        q = lax.rem(g + o, peers)
        return pltpu.make_async_remote_copy(
            src_ref=src.at[pl.ds(pl.multiple_of(q * pack, pack), pack)],
            dst_ref=dst.at[pl.ds(pl.multiple_of(g * pack, pack), pack)],
            send_sem=ssem.at[o],
            recv_sem=rsem.at[o],
            device_id=peer_id(q),
            device_id_type=MESH,
        )

    def far_arrival(o, src, dst, ssem, rsem):
        q = lax.rem(g + peers - o, peers)
        return pltpu.make_async_remote_copy(
            src_ref=src.at[pl.ds(pl.multiple_of(q * pack, pack), pack)],
            dst_ref=dst.at[pl.ds(pl.multiple_of(q * pack, pack), pack)],
            send_sem=ssem.at[o],
            recv_sem=rsem.at[o],
            device_id=peer_id(q),
            device_id_type=MESH,
        )

    def keep_own(src, dst):
        at = pl.ds(pl.multiple_of(g * pack, pack), pack)
        dst[at, :] = src[at, :]

    ahead = near_copy(0, near_src, near_in, near_ssem, near_rsem, nxt)
    behind = near_copy(1, near_src, near_in, near_ssem, near_rsem, prv)
    each_peer(lambda o: far_copy(o, far_src, far_in, far_ssem, far_rsem).start())
    ahead.start()
    behind.start()
    keep_own(far_src, far_in)

    indices[2].wait()
    indices[3].wait()
    for load in vec_loads:
        load.wait()

    loads[1].wait()
    proj_own[:n_node, :] = mm(node_bf[...], wei[d:2 * d, :]).astype(BF16)
    proj_own[n_node:, :] = mm(node_bf[...], wei[2 * d:, :]).astype(BF16)
    first_near = n_node
    first_far = n_node + 2 * near
    far_cols = proj_ghost.shape[0] - 4 * near
    for e0 in range(0, n_edge, LANES):
        scol = column_of(snd_ref, e0, LANES)
        rcol = column_of(rcv_ref, e0, LANES)
        rows = slice(e0, e0 + LANES)
        lane_ids = iota((LANES, LANES), 1)
        for c0 in range(0, n_node, LANES):
            pick_own[rows, c0:c0 + LANES] = ones_where(scol == lane_ids + c0)
            pick_own[rows, n_node + c0:n_node + c0 + LANES] = ones_where(rcol == lane_ids + c0)
        for c0 in range(0, 2 * near, LANES):
            at = first_near + c0
            pick_ghost[rows, c0:c0 + LANES] = ones_where(scol == lane_ids + at)
            pick_ghost[rows, 2 * near + c0:2 * near + c0 + LANES] = ones_where(rcol == lane_ids + at)
        for c0 in range(0, far_cols, LANES):
            c = lane_ids + c0
            is_s = c < far_rows
            slot = jnp.where(is_s, scol, rcol)
            row = jnp.where(is_s, c, c - far_rows)
            name = first_far + row % peers * far + row // peers
            pick_ghost[rows, 4 * near + c0:4 * near + c0 + LANES] = ones_where(slot == name)

    loads[2].wait()
    for e0 in range(0, n_edge, ROW_BLOCK):
        rows = slice(e0, e0 + ROW_BLOCK)
        pre[rows, :] = mm(edge_v[rows, :], wei[:d, :]) + mm(pick_own[rows, :], proj_own[...]) + ebi[...]

    rcv_row = rcv_ref[...]
    for r0, base, count in ((0, first_near, 2 * near), (lent, 0, n_node)):
        drop[r0:r0 + count, :] = ones_where(iota((count, n_edge), 0) + base == rcv_row)
    row = iota((far_rows, n_edge), 0)
    drop[2 * near:lent, :] = ones_where(first_far + row % peers * far + row // peers == rcv_row)
    if far_cols > 2 * far_rows:
        proj_ghost[4 * near + 2 * far_rows:, :] = jnp.zeros((far_cols - 2 * far_rows, d), BF16)

    each_peer(lambda o: far_arrival(o, far_src, far_in, far_ssem, far_rsem).wait_recv())
    far_nodes = unpacked(far_in[...])
    proj_ghost[4 * near:4 * near + far_rows, :] = mm(far_nodes, wei[d:2 * d, :]).astype(BF16)
    proj_ghost[4 * near + far_rows:4 * near + 2 * far_rows, :] = mm(
        far_nodes, wei[2 * d:, :]
    ).astype(BF16)
    ahead.wait_recv()
    behind.wait_recv()
    proj_ghost[:2 * near, :] = mm(near_in[...], wei[d:2 * d, :]).astype(BF16)
    proj_ghost[2 * near:4 * near, :] = mm(near_in[...], wei[2 * d:, :]).astype(BF16)

    loads[3].wait()
    stores = []
    for i, e0 in enumerate(range(0, n_edge, ROW_BLOCK)):
        rows = slice(e0, e0 + ROW_BLOCK)
        hidden = silu(pre[rows, :] + mm(pick_ghost[rows, :], proj_ghost[...])).astype(BF16)
        message = norm_rows(mm(hidden, weo[...]) + ebo[...], egain[...], eshift[...])
        msg[rows, :] = message.astype(BF16)
        edge_v[rows, :] = (edge_v[rows, :].astype(F32) + message).astype(BF16)
        store = pltpu.make_async_copy(edge_v.at[rows], edge_out.at[rows], store_sem.at[i])
        store.start()
        stores.append(store)

    near_bsrc[...] = mm(drop[:2 * near, :], msg[...]).astype(BF16)
    back_prev = near_copy(0, near_bsrc, near_back, nback_ssem, nback_rsem, prv)
    back_next = near_copy(1, near_bsrc, near_back, nback_ssem, nback_rsem, nxt)
    back_prev.start()
    back_next.start()
    far_bsrc[...] = packed(mm(drop[2 * near:lent, :], msg[...]).astype(BF16))
    each_peer(lambda o: far_copy(o, far_bsrc, far_back, fback_ssem, fback_rsem).start())
    keep_own(far_bsrc, far_back)
    own_sum[...] = mm(drop[lent:, :], msg[...])

    loads[4].wait()
    loads[5].wait()
    node_pre = mm(node_bf[...], wni[:d, :]) + nbi[...]
    give = ones_where(iota((n_node, lent), 0) == lend_ref[:, :lent])

    each_peer(lambda o: far_arrival(o, far_bsrc, far_back, fback_ssem, fback_rsem).wait_recv())
    own_sum[...] += mm(give[:, 2 * near:], unpacked(far_back[...]))
    back_prev.wait_recv()
    back_next.wait_recv()
    lane_src[...] = (own_sum[...] + mm(give[:, :2 * near], near_back[...])).astype(BF16)
    swap = pltpu.make_async_remote_copy(
        src_ref=lane_src, dst_ref=lane_in, send_sem=lane_ssem, recv_sem=lane_rsem,
        device_id={"lane": other}, device_id_type=MESH,
    )
    swap.start()
    swap.wait_recv()
    summed = (lane_src[...].astype(F32) + lane_in[...].astype(F32)).astype(BF16)
    node_hidden = silu(node_pre + mm(summed, wni[d:, :])).astype(BF16)
    node_out[...] = node_v[...] + norm_rows(
        mm(node_hidden, wno[...]) + nbo[...], ngain[...], nshift[...]
    )

    ahead.wait_send()
    behind.wait_send()
    back_prev.wait_send()
    back_next.wait_send()
    swap.wait_send()
    each_peer(lambda o: far_copy(o, far_src, far_in, far_ssem, far_rsem).wait_send())
    each_peer(lambda o: far_copy(o, far_bsrc, far_back, fback_ssem, fback_rsem).wait_send())
    for store in stores:
        store.wait()


def hand_over(node_in, edge_in, node_out, edge_out, node_v, edge_v, in_sems, out_sems):
    fetches, stores = [], []
    for a, (src, mid, dst) in enumerate(((edge_in, edge_v, edge_out), (node_in, node_v, node_out))):
        step = src.shape[0] // PIECES
        for i in range(PIECES):
            rows, at = pl.ds(i * step, step), a * PIECES + i
            fetches.append(pltpu.make_async_copy(src.at[rows], mid.at[rows], in_sems.at[at]))
            stores.append(pltpu.make_async_copy(mid.at[rows], dst.at[rows], out_sems.at[at]))
    for fetch in fetches:
        fetch.start()
    for fetch, store in zip(fetches, stores):
        fetch.wait()
        store.start()
    for store in stores:
        store.wait()


def per_device(
    node_latents, edge_latents, sender_slot, receiver_slot, near_send, far_send,
    w_edge_in, w_edge_out, w_node_in, w_node_out,
    edge_bias_in, edge_bias_out, edge_gain, edge_shift,
    node_bias_in, node_bias_out, node_gain, node_shift,
):
    n_node, d = node_latents.shape
    n_edge = edge_latents.shape[0]
    near = near_send.shape[2]
    peers, far = far_send.shape[1:]
    n_patch, n_sub, n_lane = (lax.axis_size(a) for a in ("patch", "sub", "lane"))
    far_rows = peers * far
    lent = 2 * near + far_rows
    lent_pad = -(-lent // LANES) * LANES
    ghost_k = 4 * near + -(-2 * far_rows // LANES) * LANES
    pack = far * (d // LANES)
    blocks = n_edge // ROW_BLOCK
    vectors = [v.reshape(1, d) for v in (
        edge_bias_in, edge_bias_out, edge_gain, edge_shift,
        node_bias_in, node_bias_out, node_gain, node_shift)]
    hbm = pl.BlockSpec(memory_space=pltpu.HBM)
    vmem = pl.BlockSpec(memory_space=pltpu.VMEM)
    dma = pltpu.SemaphoreType.DMA
    far_shape = (peers * pack, LANES)
    macs = n_edge * d * (3 * d + ghost_k + lent + n_node) + n_node * d * 6 * d
    results = pl.pallas_call(
        functools.partial(layer_kernel, (n_patch, n_sub, n_lane, near, far)),
        out_shape=(
            jax.ShapeDtypeStruct((n_node, d), F32),
            jax.ShapeDtypeStruct((n_edge, d), BF16),
        ),
        in_specs=[hbm] * (10 + len(vectors)),
        out_specs=(vmem, hbm),
        scratch_shapes=[
            pltpu.VMEM((1, n_edge), jnp.int32),
            pltpu.VMEM((1, n_edge), jnp.int32),
            pltpu.VMEM((1, 2 * near), jnp.int32),
            pltpu.VMEM((far, peers), jnp.int32),
            pltpu.VMEM((1, lent_pad), jnp.int32),
            pltpu.VMEM((len(vectors), 1, d), F32),
            pltpu.VMEM((n_node, d), F32),
            pltpu.VMEM((n_edge, d), BF16),
            pltpu.VMEM(w_edge_in.shape, BF16),
            pltpu.VMEM(w_edge_out.shape, BF16),
            pltpu.VMEM(w_node_in.shape, BF16),
            pltpu.VMEM(w_node_out.shape, BF16),
            pltpu.VMEM((n_node, d), BF16),
            pltpu.VMEM((lent_pad, n_node), BF16),
            pltpu.VMEM((2 * near, d), BF16),
            pltpu.VMEM(far_shape, BF16),
            pltpu.VMEM((2 * near, d), BF16),
            pltpu.VMEM(far_shape, BF16),
            pltpu.VMEM((n_edge, 2 * n_node), BF16),
            pltpu.VMEM((n_edge, ghost_k), BF16),
            pltpu.VMEM((2 * n_node, d), BF16),
            pltpu.VMEM((ghost_k, d), BF16),
            pltpu.VMEM((lent + n_node, n_edge), BF16),
            pltpu.VMEM((n_edge, d), F32),
            pltpu.VMEM((n_edge, d), BF16),
            pltpu.VMEM((2 * near, d), BF16),
            pltpu.VMEM(far_shape, BF16),
            pltpu.VMEM((2 * near, d), BF16),
            pltpu.VMEM(far_shape, BF16),
            pltpu.VMEM((n_node, d), BF16),
            pltpu.VMEM((n_node, d), BF16),
            pltpu.VMEM((n_node, d), F32),
            dma((6,)), dma((4,)), dma((len(vectors),)), dma((blocks,)),
            dma((2,)), dma((2,)), dma((peers,)), dma((peers,)),
            dma((2,)), dma((2,)), dma((peers,)), dma((peers,)),
            dma, dma,
        ],
        compiler_params=pltpu.CompilerParams(
            collective_id=0, has_side_effects=True, vmem_limit_bytes=62 * 1024 * 1024
        ),
        cost_estimate=pl.CostEstimate(
            flops=2 * macs, bytes_accessed=8 * 1024 * 1024, transcendentals=n_edge * d
        ),
        name="mesh_layer",
    )(
        node_latents, edge_latents, w_edge_in, w_edge_out, w_node_in, w_node_out,
        sender_slot.reshape(1, n_edge), receiver_slot.reshape(1, n_edge),
        near_send.reshape(1, 2 * near), jnp.swapaxes(far_send, 1, 2).reshape(far, peers), *vectors,
    )
    return tuple(pl.pallas_call(
        hand_over,
        out_shape=tuple(jax.ShapeDtypeStruct(r.shape, r.dtype) for r in results),
        in_specs=[hbm] * 2,
        out_specs=(hbm, hbm),
        scratch_shapes=[pltpu.VMEM(r.shape, r.dtype) for r in results] + [dma((2 * PIECES,))] * 2,
        compiler_params=pltpu.CompilerParams(vmem_limit_bytes=62 * 1024 * 1024),
        name="hand_over",
    )(*results))


def solution(mesh):
    nodes = P(("groups", "patch", "sub"), None)
    edges = P(("groups", "patch", "sub", "lane"), None)
    per_edge = P(("groups", "patch", "sub", "lane"))
    lists = P(("groups", "patch", "sub", "lane"), None, None)
    in_specs = (nodes, edges, per_edge, per_edge, lists, lists) + (P(),) * 12
    return jax.shard_map(
        per_device, mesh=mesh, in_specs=in_specs, out_specs=(nodes, edges), check_vma=False
    )
```
